32 devices in a mesh: groups: 2 (over x), row: 16 (over z, y, core).
Axes of the slice: x: 2, y: 2, z: 4, core: 2. Of those that a mesh axis runs over, the one named last changes fastest.
Arguments:
- homolog_features: bfloat16 [256, 256, 256], P(('groups', 'row')), parts along dimension 0, may hold values from -6 to 6
- standardize_scale: float32 [256], replicated, may hold values from 0.25 to 1.75
- standardize_shift: float32 [256], replicated, may hold values from -3 to 3
- first_factor_matrix: bfloat16 [256, 32], replicated, may hold values from -0.375 to 0.375
- first_factor_intercept: float32 [32], replicated, may hold values from -3 to 3
- second_factor_matrix: bfloat16 [256, 32], replicated, may hold values from -0.375 to 0.375
- second_factor_intercept: float32 [32], replicated, may hold values from -3 to 3
- final_mapping_matrix: bfloat16 [1024, 128], replicated, may hold values from -2 to 2
- final_mapping_intercept: float32 [128], replicated, may hold values from -3 to 3
Outputs:
- pair: bfloat16 [512, 256, 128], P(('groups', 'row')), parts along dimension 0
The draws below stay inside these ranges and needn't reach their ends.
There are 2 independent parts, one for each index of `groups`. The reference program is written for one: setup_inputs(seed, part) draws one part's arguments, and reference() takes and returns one part's arrays. A program takes and returns all parts, laid end to end along the dimension named above; an argument that names none is the same for every part. Nothing has to cross between parts.
All inputs are finite; a program needn't handle non-finite values.
Results may differ from the reference program's by a relative error of at most 0.0054.
Values may be sent and summed in bfloat16 or wider, within the bound.
A program may use at most 128 MiB of HBM per device.

```python
import jax
import jax.numpy as jnp
from jax import lax

ALIGNED_HOMOLOGS = 128
ALIGN_FEATURES = 256
HIDDEN_WIDTH = 32
CZ = 128
ROWS_DEV = 16
CHAIN_LENGTH = 256
N_ROW = 16


def block_levels(own_key, dims, shards, smallest, top_value):
    level = 1.0
    for dim, shards_of in shards:
        heights = jax.random.uniform(jax.random.fold_in(jax.random.fold_in(own_key, 6), dim), (shards_of,), jnp.float32, smallest / len(shards), top_value / len(shards))
        level = level * jnp.repeat(jnp.exp(heights), dims[dim] // shards_of).reshape((-1,) + (1,) * (len(dims) - 1 - dim))
    return level


def normal_values(rng, shape, scale, most, pieces=(), held_as=jnp.bfloat16):
    level = block_levels(rng, shape, pieces, -0.22, 0.18) if pieces else 1.0
    values = jax.random.normal(rng, shape, jnp.float32) * scale * level
    return jnp.minimum(jnp.maximum(values, -most), most).astype(held_as)


def setup_inputs(seed: int = 0, part: int = 0) -> dict:
    key_of = jax.random.split(jax.random.key(seed), 10)
    part_splits = jax.random.split(jax.random.fold_in(key_of[9], part), 10)
    homolog_features = normal_values(part_splits[0], (ALIGNED_HOMOLOGS, CHAIN_LENGTH, ALIGN_FEATURES), 1.0, 6.0, ((0, 16),))
    standardize_scale = jnp.clip(1.0 + 0.15 * jax.random.normal(key_of[1], (ALIGN_FEATURES,), jnp.float32), 0.25, 1.75)
    standardize_shift = normal_values(key_of[2], (ALIGN_FEATURES,), 0.3, 3.0, (), jnp.float32)
    first_factor_matrix = normal_values(key_of[3], (ALIGN_FEATURES, HIDDEN_WIDTH), ALIGN_FEATURES ** -0.5, 0.375)
    first_factor_intercept = normal_values(key_of[4], (HIDDEN_WIDTH,), 0.5, 3.0, (), jnp.float32)
    second_factor_matrix = normal_values(key_of[5], (ALIGN_FEATURES, HIDDEN_WIDTH), ALIGN_FEATURES ** -0.5, 0.375)
    second_factor_intercept = normal_values(key_of[6], (HIDDEN_WIDTH,), 0.5, 3.0, (), jnp.float32)
    final_mapping_matrix = normal_values(key_of[7], (HIDDEN_WIDTH * HIDDEN_WIDTH, CZ), 0.35, 2.0)
    final_mapping_intercept = normal_values(key_of[8], (CZ,), 0.5, 3.0, (), jnp.float32)
    return dict(homolog_features=homolog_features, standardize_scale=standardize_scale, standardize_shift=standardize_shift, first_factor_matrix=first_factor_matrix, first_factor_intercept=first_factor_intercept, second_factor_matrix=second_factor_matrix, second_factor_intercept=second_factor_intercept, final_mapping_matrix=final_mapping_matrix, final_mapping_intercept=final_mapping_intercept)


def build_factor_pairs(homolog_features, standardize_scale, standardize_shift, first_factor_matrix, first_factor_intercept, second_factor_matrix, second_factor_intercept):
    element_quantities = homolog_features.astype(jnp.float32)
    average = lax.optimization_barrier(jnp.mean(element_quantities, axis=-1, keepdims=True))
    centered = element_quantities - average
    variance = lax.optimization_barrier(jnp.mean(centered * centered, axis=-1, keepdims=True))
    normed = (centered * lax.rsqrt(variance + 1e-05) * standardize_scale + standardize_shift).astype(jnp.bfloat16)
    flattened = normed.reshape(-1, normed.shape[-1])
    first_factor_rows = (jnp.dot(flattened, first_factor_matrix, preferred_element_type=jnp.float32) + first_factor_intercept).astype(jnp.bfloat16)
    second_factor_rows = (jnp.dot(flattened, second_factor_matrix, preferred_element_type=jnp.float32) + second_factor_intercept).astype(jnp.bfloat16)
    tensor_shape_info = (homolog_features.shape[0], homolog_features.shape[1], first_factor_matrix.shape[1])
    return (first_factor_rows.reshape(tensor_shape_info), second_factor_rows.reshape(tensor_shape_info))

def reference(homolog_features, standardize_scale, standardize_shift, first_factor_matrix, first_factor_intercept, second_factor_matrix, second_factor_intercept, final_mapping_matrix, final_mapping_intercept):
    first_factor_rows, second_factor_rows = build_factor_pairs(homolog_features, standardize_scale, standardize_shift, first_factor_matrix, first_factor_intercept, second_factor_matrix, second_factor_intercept)
    right_wide = second_factor_rows.astype(jnp.float32)

    def row_block(start):
        rows = lax.dynamic_slice_in_dim(first_factor_rows, start, ROWS_DEV, 1).astype(jnp.float32)
        outer = jnp.einsum('sic,sje->ijce', rows, right_wide) / ALIGNED_HOMOLOGS
        outer = outer.astype(jnp.bfloat16).reshape(ROWS_DEV * CHAIN_LENGTH, HIDDEN_WIDTH * HIDDEN_WIDTH)
        result = jnp.dot(outer, final_mapping_matrix, preferred_element_type=jnp.float32) + final_mapping_intercept
        return result.astype(jnp.bfloat16).reshape(ROWS_DEV, CHAIN_LENGTH, CZ)
    starts = (jnp.arange(N_ROW, dtype=jnp.int32) * ROWS_DEV).astype(jnp.int32)
    stacked = lax.map(row_block, starts)
    return stacked.reshape(CHAIN_LENGTH, CHAIN_LENGTH, CZ)
```

```python
import functools

import jax
import jax.numpy as jnp
from jax import lax
from jax.experimental import pallas as pl
from jax.experimental.pallas import tpu as pltpu
from jax.sharding import PartitionSpec as P

LANES = 128
ROWS16 = 16


class Sizes:
    def __init__(self, n, seqs, residues, width, cz):
        self.n = n
        self.seqs = seqs
        self.res = residues
        self.width = width
        self.cz = cz
        self.own = residues // n
        self.parts = ROWS16 // seqs
        self.eper = width // self.parts
        self.chunks = residues // LANES
        self.tiles = self.chunks * self.eper
        self.pack = LANES // width
        self.groups = self.own // self.pack
        self.ghigh = min(self.parts, self.groups)
        self.q = self.groups // self.ghigh
        self.k = n * ROWS16


def project(z, x_ref, scale_ref, shift_ref, w1_ref, b1_ref, w2_ref, b2_ref, wide, tall):
    w1 = jnp.concatenate([w1_ref[...]] * z.pack, axis=1)
    b1 = jnp.concatenate([b1_ref[...]] * z.pack, axis=1)
    w2t = w2_ref[...].astype(jnp.float32).T.astype(jnp.bfloat16)
    eye = lax.broadcasted_iota(jnp.int32, (z.width, z.width), 0) == lax.broadcasted_iota(
        jnp.int32, (z.width, z.width), 1
    )
    b2 = jnp.sum(jnp.where(eye, b2_ref[...], 0.0), axis=1, keepdims=True)
    scale = scale_ref[...]
    shift = shift_ref[...]
    for s in range(z.seqs):
        x = x_ref[s].astype(jnp.float32)
        average = jnp.mean(x, axis=-1, keepdims=True)
        centered = x - average
        variance = jnp.mean(centered * centered, axis=-1, keepdims=True)
        normed = (centered * lax.rsqrt(variance + 1e-05) * scale + shift).astype(jnp.bfloat16)
        tall[pl.ds(s * z.res, z.res), :] = (
            jnp.dot(normed, w1, preferred_element_type=jnp.float32) + b1
        )
        right = (
            lax.dot_general(
                w2t, normed, (((1,), (1,)), ((), ())), preferred_element_type=jnp.float32
            )
            + b2
        )
        for h in range(z.parts):
            for c in range(z.chunks):
                wide[pl.ds(c * z.eper * ROWS16 + h * z.seqs + s, z.eper, stride=ROWS16), :] = right[
                    h * z.eper : (h + 1) * z.eper, c * LANES : (c + 1) * LANES
                ]


def pack_left(z, tall, flat, block_ref):
    if z.ghigh * z.seqs < ROWS16:
        flat[...] = jnp.zeros_like(flat)
    lane = lax.broadcasted_iota(jnp.int32, (z.seqs, LANES), 1) // z.width
    for r in range(z.n):
        for g in range(z.groups):
            first = r * z.own + g * z.pack
            value = tall[pl.ds(first, z.seqs, stride=z.res), :]
            for p in range(1, z.pack):
                value = jnp.where(lane == p, tall[pl.ds(first + p, z.seqs, stride=z.res), :], value)
            q, gh = g // z.ghigh, g % z.ghigh
            flat[pl.ds((r * z.q + q) * ROWS16 + gh * z.seqs, z.seqs), :] = value
    block_ref[...] = flat[...].reshape(block_ref.shape).astype(jnp.bfloat16)


def spread_left(z, left_ref, a_ref):
    for q in range(z.q):
        block = left_ref[:, q].reshape(z.k, LANES).astype(jnp.float32).T
        part = (lax.broadcasted_iota(jnp.int32, block.shape, 1) // z.seqs) % z.parts
        for gh in range(z.ghigh):
            for h in range(z.parts):
                turn = ((h - gh) * z.seqs) % z.k
                moved = pltpu.roll(block, turn, 1) if turn else block
                first = h * z.own * z.width + (q * z.ghigh + gh) * LANES
                a_ref[pl.ds(first, LANES), :] = jnp.where(part == h, moved, 0.0).astype(jnp.bfloat16)


def turn_weights(z, w_ref, wide, wt_ref):
    wide[...] = w_ref[...].astype(jnp.float32)
    for e in range(z.width):
        rows = wide[pl.ds(e, z.width, stride=z.width), :]
        if e % z.pack == 0:
            held = []
        held.append(rows)
        if e % z.pack == z.pack - 1:
            first = (e - z.pack + 1) * z.width
            wt_ref[:, first : first + LANES] = jnp.concatenate(held, axis=0).T.astype(jnp.bfloat16)


def outer_chunk(z, c, a_ref, gathered, held):
    def body(pair, carry):
        tile = c * z.eper + 2 * pair
        b = jnp.concatenate(
            [gathered[:, tile + t].reshape(z.k, LANES) for t in range(2)], axis=1
        )
        for h in range(z.parts):
            o = jnp.dot(
                a_ref[pl.ds(h * z.own * z.width, z.own * z.width), :],
                b,
                preferred_element_type=jnp.float32,
            ).astype(jnp.bfloat16)
            for t in range(2):
                first = pl.multiple_of((h * z.eper + 2 * pair + t) * z.width, z.width)
                for i in range(z.own):
                    held[i // 2, pl.ds(first, z.width), pl.ds((i % 2) * LANES, LANES)] = o[
                        i * z.width : (i + 1) * z.width, t * LANES : (t + 1) * LANES
                    ]
        return carry

    lax.fori_loop(0, z.eper // 2, body, 0)


def map_chunk(z, c, inverse, wt_ref, bias_ref, held, out_ref):
    bias = bias_ref[...]

    def body(pair, carry):
        result = jnp.dot(wt_ref[...], held[pair], preferred_element_type=jnp.float32)
        for t in range(2):
            value = result[:, t * LANES : (t + 1) * LANES].T * inverse + bias
            out_ref[2 * pair + t, pl.ds(c * LANES, LANES), :] = value.astype(jnp.bfloat16)
        return carry

    lax.fori_loop(0, z.own // 2, body, 0)


def project_kernel(z, x, scale, shift, w1, b1, w2, b2, right_ref, left_ref, wide, tall, flat):
    project(z, x, scale, shift, w1, b1, w2, b2, wide, tall)
    right_ref[...] = wide[...].reshape(right_ref.shape).astype(jnp.bfloat16)
    pack_left(z, tall, flat, left_ref)


def pair_kernel(z, inverse, gathered, left, w, bias, out_ref, wide, wt, a, held):
    turn_weights(z, w, wide, wt)
    spread_left(z, left, a)
    for c in range(z.chunks):
        outer_chunk(z, c, a, gathered, held)
        map_chunk(z, c, inverse, wt, bias, held, out_ref)


def solution(mesh):
    n = mesh.shape["row"]
    vmem = pl.BlockSpec(memory_space=pltpu.VMEM)

    def local(x, scale, shift, w1, b1, w2, b2, w, bias):
        z = Sizes(n, x.shape[0], x.shape[1], w1.shape[1], w.shape[1])
        inverse = 1.0 / (n * x.shape[0])
        right, left = pl.pallas_call(
            functools.partial(project_kernel, z),
            out_shape=(
                jax.ShapeDtypeStruct((z.tiles, ROWS16, LANES), jnp.bfloat16),
                jax.ShapeDtypeStruct((n, z.q, ROWS16, LANES), jnp.bfloat16),
            ),
            in_specs=[vmem] * 7,
            out_specs=(vmem, vmem),
            scratch_shapes=[
                pltpu.VMEM((z.tiles * ROWS16, LANES), jnp.float32),
                pltpu.VMEM((z.seqs * z.res, LANES), jnp.float32),
                pltpu.VMEM((n * z.q * ROWS16, LANES), jnp.float32),
            ],
            compiler_params=pltpu.CompilerParams(vmem_limit_bytes=48 * 2**20),
        )(x, scale.reshape(1, -1), shift.reshape(1, -1), w1, b1.reshape(1, -1), w2, b2.reshape(1, -1))
        left = lax.all_to_all(left, "row", split_axis=0, concat_axis=0, tiled=True)
        gathered = lax.all_gather(right, "row", axis=0, tiled=False)
        return pl.pallas_call(
            functools.partial(pair_kernel, z, inverse),
            out_shape=jax.ShapeDtypeStruct((z.own, z.res, z.cz), jnp.bfloat16),
            in_specs=[vmem] * 4,
            out_specs=vmem,
            scratch_shapes=[
                pltpu.VMEM(w.shape, jnp.float32),
                pltpu.VMEM((z.cz, w.shape[0]), jnp.bfloat16),
                pltpu.VMEM((z.parts * z.own * z.width, z.k), jnp.bfloat16),
                pltpu.VMEM((z.own // 2, z.width * z.width, 2 * LANES), jnp.bfloat16),
            ],
            compiler_params=pltpu.CompilerParams(vmem_limit_bytes=56 * 2**20),
        )(gathered, left, w, bias.reshape(1, -1))

    in_specs = (P(("groups", "row"), None, None), P(), P(), P(), P(), P(), P(), P(), P())
    return jax.shard_map(
        local,
        mesh=mesh,
        in_specs=in_specs,
        out_specs=P(("groups", "row"), None, None),
        check_vma=False,
    )
```

```python
import functools

import jax
import jax.numpy as jnp
from jax import lax
from jax.experimental import pallas as pl
from jax.experimental.pallas import tpu as pltpu
from jax.sharding import PartitionSpec as P

LANES = 128
ROWS16 = 16
CONTRACT_LAST = (((1,), (1,)), ((), ()))
MESH = pl.DeviceIdType.MESH


class Sizes:
    def __init__(self, n, seqs, residues, width, cz):
        self.n = n
        self.seqs = seqs
        self.res = residues
        self.width = width
        self.cz = cz
        self.own = residues // n
        self.parts = ROWS16 // seqs
        self.eper = width // self.parts
        self.chunks = residues // LANES
        self.tiles = self.chunks * self.eper
        self.pack = LANES // width
        self.groups = self.own // self.pack
        self.ghigh = min(self.parts, self.groups)
        self.q = self.groups // self.ghigh
        self.k = n * ROWS16
        self.half = self.eper // 2
        self.waves = min(2, self.chunks)
        self.per_wave = self.chunks // self.waves
        self.piece = self.per_wave * self.half
        self.chips = n // 2
        self.hops = self.chips // 2

    def tile(self, chunk, u):
        wave, at = divmod(chunk, self.per_wave)
        return ((wave * 2 + u) * self.per_wave + at) * self.half


def project(z, wave, x_ref, params, wide, tall):
    w1, b1, w2, b2, scale, shift = params
    count = z.per_wave * LANES
    for s in range(z.seqs):
        x = x_ref[s, wave * count : (wave + 1) * count, :].astype(jnp.float32)
        average = jnp.mean(x, axis=-1, keepdims=True)
        centered = x - average
        variance = jnp.mean(centered * centered, axis=-1, keepdims=True)
        normed = (centered * lax.rsqrt(variance + 1e-05) * scale + shift).astype(jnp.bfloat16)
        tall[pl.ds(s * z.res + wave * count, count), :] = (
            lax.dot_general(normed, w1, CONTRACT_LAST, preferred_element_type=jnp.float32) + b1
        )
        right = (
            lax.dot_general(w2, normed, CONTRACT_LAST, preferred_element_type=jnp.float32) + b2
        )
        for h in range(z.parts):
            for at in range(z.per_wave):
                for u in range(2):
                    row = z.tile(wave * z.per_wave + at, u) * ROWS16 + h * z.seqs + s
                    first = h * z.eper + u * z.half
                    wide[pl.ds(row, z.half, stride=ROWS16), :] = right[
                        first : first + z.half, at * LANES : (at + 1) * LANES
                    ]


def pack_left(z, tall, flat, block_ref):
    if z.ghigh * z.seqs < ROWS16:
        flat[...] = jnp.zeros_like(flat)
    lane = lax.broadcasted_iota(jnp.int32, (z.seqs, LANES), 1) // z.width
    for r in range(z.n):
        for g in range(z.groups):
            first = r * z.own + g * z.pack
            value = tall[pl.ds(first, z.seqs, stride=z.res), :]
            for p in range(1, z.pack):
                value = jnp.where(lane == p, tall[pl.ds(first + p, z.seqs, stride=z.res), :], value)
            q, gh = g // z.ghigh, g % z.ghigh
            flat[pl.ds((r * z.q + q) * ROWS16 + gh * z.seqs, z.seqs), :] = value
    block_ref[...] = flat[...].reshape(block_ref.shape).astype(jnp.bfloat16)


def spread_left(z, left_ref, a_ref):
    for q in range(z.q):
        block = left_ref[:, q].reshape(z.k, LANES).astype(jnp.float32).T
        part = (lax.broadcasted_iota(jnp.int32, block.shape, 1) // z.seqs) % z.parts
        for gh in range(z.ghigh):
            for h in range(z.parts):
                turn = ((h - gh) * z.seqs) % z.k
                moved = pltpu.roll(block, turn, 1) if turn else block
                first = h * z.own * z.width + (q * z.ghigh + gh) * LANES
                a_ref[pl.ds(first, LANES), :] = jnp.where(part == h, moved, 0.0).astype(jnp.bfloat16)


def turn_weights(z, w_ref, wide, wt_ref):
    wide[...] = w_ref[...].astype(jnp.float32)
    for e in range(z.width):
        rows = wide[pl.ds(e, z.width, stride=z.width), :]
        if e % z.pack == 0:
            held = []
        held.append(rows)
        if e % z.pack == z.pack - 1:
            first = (e - z.pack + 1) * z.width
            wt_ref[:, first : first + LANES] = jnp.concatenate(held, axis=0).T.astype(jnp.bfloat16)


def outer_part(z, c, u, a_ref, gathered, held):
    def body(pair, carry):
        tile = z.tile(c, u) + 2 * pair
        b = jnp.concatenate(
            [gathered[:, tile + t].reshape(z.k, LANES) for t in range(2)], axis=1
        )
        for h in range(z.parts):
            o = jnp.dot(
                a_ref[pl.ds(h * z.own * z.width, z.own * z.width), :],
                b,
                preferred_element_type=jnp.float32,
            ).astype(jnp.bfloat16)
            for t in range(2):
                first = pl.multiple_of(
                    (h * z.eper + u * z.half + 2 * pair + t) * z.width, z.width
                )
                for i in range(z.own):
                    held[i // 2, pl.ds(first, z.width), pl.ds((i % 2) * LANES, LANES)] = o[
                        i * z.width : (i + 1) * z.width, t * LANES : (t + 1) * LANES
                    ]
        return carry

    lax.fori_loop(0, z.half // 2, body, 0)


def map_part(z, c, u, inverse, wt_ref, bias_ref, held, out_ref):
    bias = bias_ref[...]

    def body(pair, carry):
        result = jnp.dot(wt_ref[...], held[pair], preferred_element_type=jnp.float32)
        for t in range(2):
            value = result[:, t * LANES : (t + 1) * LANES].T * inverse + bias
            out_ref[2 * pair + t, pl.ds(c * LANES, LANES), :] = value.astype(jnp.bfloat16)
        return carry

    pairs = z.own // 2
    lax.fori_loop(u * pairs // 2, (u + 1) * pairs // 2, body, 0)


def kernel(z, inverse, *refs):
    hbm, out_ref = refs[:9], refs[9]
    local_refs = refs[10:19]
    wide, tall, flat, packed, left, gathered, wide_w, wt, a, held = refs[19:29]
    load_sem, ring_send, ring_recv, sib_send, sib_recv, left_send, left_recv = refs[29:]
    x, scale, shift, w1, b1, w2, b2, w, bias = local_refs

    me = lax.axis_index("row")
    core, chip = lax.rem(me, 2), me // 2
    place = jnp.where(lax.rem(chip, 2) == 0, chip // 2, z.chips - 1 - chip // 2)

    def device_at(p):
        p = lax.rem(p + z.chips, z.chips)
        at = jnp.where(p < z.chips // 2, 2 * p, 2 * (z.chips - 1 - p) + 1)
        return at * 2 + core

    ahead, behind, sibling = device_at(place + 1), device_at(place - 1), me + 1 - 2 * core

    loads = [
        pltpu.make_async_copy(hbm[k], local_refs[k], load_sem.at[k]) for k in range(1, 9)
    ]
    count = z.per_wave * LANES
    x_loads = [
        pltpu.make_async_copy(
            hbm[0].at[:, pl.ds(v * count, count)],
            x.at[:, pl.ds(v * count, count)],
            load_sem.at[9 + v],
        )
        for v in range(z.waves)
    ]
    x_loads[0].start()
    for load in loads:
        load.start()
    for load in x_loads[1:]:
        load.start()
    barrier = pltpu.get_barrier_semaphore()
    for k in range(1, z.n):
        pl.semaphore_signal(
            barrier, inc=1, device_id={"row": lax.rem(me + k, z.n)}, device_id_type=MESH
        )

    def ring(direction, hop, p, source):
        part = gathered.at[source, pl.ds(p * z.piece, z.piece)]
        return pltpu.make_async_remote_copy(
            src_ref=part,
            dst_ref=part,
            send_sem=ring_send.at[direction, hop - 1, p],
            recv_sem=ring_recv.at[direction, hop - 1, p],
            device_id={"row": (ahead, behind)[direction]},
            device_id_type=MESH,
        )

    def across(key, p, source):
        part = gathered.at[source, pl.ds(p * z.piece, z.piece)]
        return pltpu.make_async_remote_copy(
            src_ref=part,
            dst_ref=part,
            send_sem=sib_send.at[key, p],
            recv_sem=sib_recv.at[key, p],
            device_id={"row": sibling},
            device_id_type=MESH,
        )

    def to_owner(k):
        return pltpu.make_async_remote_copy(
            src_ref=packed.at[lax.rem(me + k, z.n)],
            dst_ref=left.at[me],
            send_sem=left_send.at[k],
            recv_sem=left_recv.at[k],
            device_id={"row": lax.rem(me + k, z.n)},
            device_id_type=MESH,
        )

    started = []

    def start(copy):
        copy.start()
        started.append(copy)

    def travels(direction, hop, u):
        return hop < z.hops or (hop == z.hops and u == direction)

    def send_own(wave):
        for u in range(2):
            for direction in range(2):
                if travels(direction, 1, u):
                    start(ring(direction, 1, wave * 2 + u, me))

    def send_across(wave):
        for u in range(2):
            start(across(0, wave * 2 + u, me))

    def pass_on(wave, hop):
        for u in range(2):
            for direction in range(2):
                if not travels(direction, hop, u):
                    continue
                p = wave * 2 + u
                source = device_at(place + (hop if direction else z.chips - hop))
                ring(direction, hop, p, source).wait_recv()
                if travels(direction, hop + 1, u):
                    start(ring(direction, hop + 1, p, source))
                key = hop if direction == 0 or hop == z.hops else z.hops + hop
                start(across(key, p, source))

    def wait_across(p):
        for key in range(z.chips):
            step = key if key <= z.hops else z.hops - key
            source = device_at(place - step + z.chips) + 1 - 2 * core
            across(key, p, source).wait_recv()

    for load in loads:
        load.wait()
    w1t = jnp.concatenate([w1[...]] * z.pack, axis=0)
    b1_wide = jnp.concatenate([b1[...]] * z.pack, axis=1)
    eye = lax.broadcasted_iota(jnp.int32, (z.width, z.width), 0) == lax.broadcasted_iota(
        jnp.int32, (z.width, z.width), 1
    )
    b2_tall = jnp.sum(jnp.where(eye, b2[...], 0.0), axis=1, keepdims=True)
    params = (w1t, b1_wide, w2[...], b2_tall, scale[...], shift[...])
    rows = 2 * z.piece
    for wave in range(z.waves):
        x_loads[wave].wait()
        project(z, wave, x, params, wide, tall)
        part = wide[pl.ds(wave * rows * ROWS16, rows * ROWS16), :]
        gathered[me, pl.ds(wave * rows, rows)] = part.reshape(rows, ROWS16, LANES).astype(jnp.bfloat16)
        if wave == 0:
            pl.semaphore_wait(barrier, z.n - 1)
            send_own(0)
            send_across(0)
    pack_left(z, tall, flat, packed)
    for k in range(1, z.n):
        start(to_owner(k))
    left[me] = packed[me]
    pass_on(0, 1)
    turn_weights(z, w, wide_w, wt)
    for hop in range(2, z.hops + 1):
        pass_on(0, hop)
        if hop == 2:
            for wave in range(1, z.waves):
                send_own(wave)
                send_across(wave)
    for k in range(1, z.n):
        pltpu.make_async_remote_copy(
            src_ref=packed.at[me],
            dst_ref=left.at[lax.rem(me - k + z.n, z.n)],
            send_sem=left_send.at[k],
            recv_sem=left_recv.at[k],
            device_id={"row": lax.rem(me + k, z.n)},
            device_id_type=MESH,
        ).wait_recv()
    spread_left(z, left, a)

    for wave in range(z.waves):
        pending = list(range(1, z.hops + 1)) if wave + 1 < z.waves else []
        items = z.per_wave * 4
        each = -(-len(pending) // items)
        waited = set()
        for at in range(z.per_wave):
            c = wave * z.per_wave + at
            for item in range(4):
                for hop in pending[:each]:
                    pass_on(wave + 1, hop)
                pending = pending[each:]
                u = item % 2
                if item < 2:
                    if u not in waited:
                        waited.add(u)
                        wait_across(wave * 2 + u)
                    outer_part(z, c, u, a, gathered, held)
                else:
                    map_part(z, c, u, inverse, wt, bias, held, out_ref)
    for copy in started:
        copy.wait_send()


def solution(mesh):
    n = mesh.shape["row"]
    vmem = pl.BlockSpec(memory_space=pltpu.VMEM)

    def local(x, scale, shift, w1, b1, w2, b2, w, bias):
        z = Sizes(n, x.shape[0], x.shape[1], w1.shape[1], w.shape[1])
        inverse = 1.0 / (n * x.shape[0])
        pieces = 2 * z.waves
        operands = (
            x, scale.reshape(1, -1), shift.reshape(1, -1), w1.T, b1.reshape(1, -1),
            w2.T, b2.reshape(1, -1), w, bias.reshape(1, -1),
        )
        dma = pltpu.SemaphoreType.DMA
        bf16, f32 = jnp.bfloat16, jnp.float32
        return pl.pallas_call(
            functools.partial(kernel, z, inverse),
            out_shape=jax.ShapeDtypeStruct((z.own, z.res, z.cz), bf16),
            in_specs=[pl.BlockSpec(memory_space=pl.ANY)] * 9,
            out_specs=vmem,
            scratch_shapes=[pltpu.VMEM(o.shape, o.dtype) for o in operands]
            + [
                pltpu.VMEM((z.tiles * ROWS16, LANES), f32),
                pltpu.VMEM((z.seqs * z.res, LANES), f32),
                pltpu.VMEM((n * z.q * ROWS16, LANES), f32),
                pltpu.VMEM((n, z.q, ROWS16, LANES), bf16),
                pltpu.VMEM((n, z.q, ROWS16, LANES), bf16),
                pltpu.VMEM((n, z.tiles, ROWS16, LANES), bf16),
                pltpu.VMEM(w.shape, f32),
                pltpu.VMEM((z.cz, w.shape[0]), bf16),
                pltpu.VMEM((z.parts * z.own * z.width, z.k), bf16),
                pltpu.VMEM((z.own // 2, z.width * z.width, 2 * LANES), bf16),
                dma((9 + z.waves,)),
                dma((2, z.hops, pieces)),
                dma((2, z.hops, pieces)),
                dma((z.chips, pieces)),
                dma((z.chips, pieces)),
                dma((n,)),
                dma((n,)),
            ],
            compiler_params=pltpu.CompilerParams(
                vmem_limit_bytes=56 * 2**20, collective_id=0, has_side_effects=True
            ),
        )(*operands)

    in_specs = (P(("groups", "row"), None, None), P(), P(), P(), P(), P(), P(), P(), P())
    return jax.shard_map(
        local,
        mesh=mesh,
        in_specs=in_specs,
        out_specs=P(("groups", "row"), None, None),
        check_vma=False,
    )
```

```python
import functools

import jax
import jax.numpy as jnp
from jax import lax
from jax.experimental import pallas as pl
from jax.experimental.pallas import tpu as pltpu
from jax.sharding import PartitionSpec as P

LANES = 128
ROWS16 = 16
CONTRACT_LAST = (((1,), (1,)), ((), ()))
MESH = pl.DeviceIdType.MESH


class Sizes:
    def __init__(self, n, seqs, residues, width, cz):
        self.n = n
        self.seqs = seqs
        self.res = residues
        self.width = width
        self.cz = cz
        self.own = residues // n
        self.parts = ROWS16 // seqs
        self.eper = width // self.parts
        self.chunks = residues // LANES
        self.tiles = self.chunks * self.eper
        self.pack = LANES // width
        self.groups = self.own // self.pack
        self.ghigh = min(self.parts, self.groups)
        self.q = self.groups // self.ghigh
        self.k = n * ROWS16
        self.half = self.eper // 2
        self.waves = 2
        self.per_wave = self.chunks // self.waves
        self.piece = self.per_wave * self.eper
        self.chips = n // 2
        self.hops = self.chips // 2

    def tile(self, chunk, u):
        return chunk * self.eper + u * self.half


def project(z, wave, x_ref, params, wide, tall):
    w1, b1, w2, b2, scale, shift = params
    count = z.per_wave * LANES
    for s in range(z.seqs):
        x = x_ref[s, wave * count : (wave + 1) * count, :].astype(jnp.float32)
        average = jnp.mean(x, axis=-1, keepdims=True)
        centered = x - average
        variance = jnp.mean(centered * centered, axis=-1, keepdims=True)
        normed = (centered * lax.rsqrt(variance + 1e-05) * scale + shift).astype(jnp.bfloat16)
        tall[pl.ds(s * z.res + wave * count, count), :] = (
            lax.dot_general(normed, w1, CONTRACT_LAST, preferred_element_type=jnp.float32) + b1
        )
        right = (
            lax.dot_general(w2, normed, CONTRACT_LAST, preferred_element_type=jnp.float32) + b2
        )
        for h in range(z.parts):
            for at in range(z.per_wave):
                for u in range(2):
                    row = z.tile(wave * z.per_wave + at, u) * ROWS16 + h * z.seqs + s
                    first = h * z.eper + u * z.half
                    wide[pl.ds(row, z.half, stride=ROWS16), :] = right[
                        first : first + z.half, at * LANES : (at + 1) * LANES
                    ]


def pack_left(z, tall, flat, block_ref):
    if z.ghigh * z.seqs < ROWS16:
        flat[...] = jnp.zeros_like(flat)
    lane = lax.broadcasted_iota(jnp.int32, (z.seqs, LANES), 1) // z.width
    for r in range(z.n):
        for g in range(z.groups):
            first = r * z.own + g * z.pack
            value = tall[pl.ds(first, z.seqs, stride=z.res), :]
            for p in range(1, z.pack):
                value = jnp.where(lane == p, tall[pl.ds(first + p, z.seqs, stride=z.res), :], value)
            q, gh = g // z.ghigh, g % z.ghigh
            flat[pl.ds((r * z.q + q) * ROWS16 + gh * z.seqs, z.seqs), :] = value
    block_ref[...] = flat[...].reshape(block_ref.shape).astype(jnp.bfloat16)


def spread_left(z, left_ref, a_ref):
    for q in range(z.q):
        block = left_ref[:, q].reshape(z.k, LANES).astype(jnp.float32).T
        part = (lax.broadcasted_iota(jnp.int32, block.shape, 1) // z.seqs) % z.parts
        for gh in range(z.ghigh):
            for h in range(z.parts):
                turn = ((h - gh) * z.seqs) % z.k
                moved = pltpu.roll(block, turn, 1) if turn else block
                first = h * z.own * z.width + (q * z.ghigh + gh) * LANES
                a_ref[pl.ds(first, LANES), :] = jnp.where(part == h, moved, 0.0).astype(jnp.bfloat16)


def turn_weights(z, w_ref, wide, wt_ref):
    wide[...] = w_ref[...].astype(jnp.float32)
    for e in range(z.width):
        rows = wide[pl.ds(e, z.width, stride=z.width), :]
        if e % z.pack == 0:
            held = []
        held.append(rows)
        if e % z.pack == z.pack - 1:
            first = (e - z.pack + 1) * z.width
            wt_ref[:, first : first + LANES] = jnp.concatenate(held, axis=0).T.astype(jnp.bfloat16)


def outer_part(z, c, u, a_ref, gathered, held):
    def body(pair, carry):
        tile = z.tile(c, u) + 2 * pair
        b = jnp.concatenate(
            [gathered[:, tile + t].reshape(z.k, LANES) for t in range(2)], axis=1
        )
        for h in range(z.parts):
            o = jnp.dot(
                a_ref[pl.ds(h * z.own * z.width, z.own * z.width), :],
                b,
                preferred_element_type=jnp.float32,
            ).astype(jnp.bfloat16)
            for t in range(2):
                first = pl.multiple_of(
                    (h * z.eper + u * z.half + 2 * pair + t) * z.width, z.width
                )
                for i in range(z.own):
                    held[i // 2, pl.ds(first, z.width), pl.ds((i % 2) * LANES, LANES)] = o[
                        i * z.width : (i + 1) * z.width, t * LANES : (t + 1) * LANES
                    ]
        return carry

    lax.fori_loop(0, z.half // 2, body, 0, unroll=True)


def map_part(z, c, u, inverse, wt_ref, bias_ref, held, out_ref):
    bias = bias_ref[...]

    def body(pair, carry):
        result = jnp.dot(wt_ref[...], held[pair], preferred_element_type=jnp.float32)
        for t in range(2):
            value = result[:, t * LANES : (t + 1) * LANES].T * inverse + bias
            out_ref[2 * pair + t, pl.ds(c * LANES, LANES), :] = value.astype(jnp.bfloat16)
        return carry

    pairs = z.own // 2
    lax.fori_loop(u * pairs // 2, (u + 1) * pairs // 2, body, 0, unroll=True)


def kernel(z, inverse, *refs):
    hbm, out_ref = refs[:9], refs[9]
    local_refs = refs[10:19]
    wide, tall, flat, packed, left, gathered, wide_w, wt, a, held = refs[19:29]
    load_sem, ring_send, ring_recv, sib_send, sib_recv, left_send, left_recv = refs[29:]
    x, scale, shift, w1, b1, w2, b2, w, bias = local_refs

    me = lax.axis_index("row")
    core, chip = lax.rem(me, 2), me // 2
    place = jnp.where(lax.rem(chip, 2) == 0, chip // 2, z.chips - 1 - chip // 2)

    def device_at(p):
        p = lax.rem(p + z.chips, z.chips)
        at = jnp.where(p < z.chips // 2, 2 * p, 2 * (z.chips - 1 - p) + 1)
        return at * 2 + core

    ahead, behind, sibling = device_at(place + 1), device_at(place - 1), me + 1 - 2 * core

    loads = [
        pltpu.make_async_copy(hbm[k], local_refs[k], load_sem.at[k]) for k in range(1, 9)
    ]
    count = z.per_wave * LANES
    x_loads = [
        pltpu.make_async_copy(
            hbm[0].at[:, pl.ds(v * count, count)],
            x.at[:, pl.ds(v * count, count)],
            load_sem.at[9 + v],
        )
        for v in range(z.waves)
    ]
    x_loads[0].start()
    for load in loads:
        load.start()
    for load in x_loads[1:]:
        load.start()
    barrier = pltpu.get_barrier_semaphore()
    for k in range(1, z.n):
        pl.semaphore_signal(
            barrier, inc=1, device_id={"row": lax.rem(me + k, z.n)}, device_id_type=MESH
        )

    def ring(direction, hop, p, source):
        part = gathered.at[source, pl.ds(p * z.piece, z.piece)]
        return pltpu.make_async_remote_copy(
            src_ref=part,
            dst_ref=part,
            send_sem=ring_send.at[direction, hop - 1, p],
            recv_sem=ring_recv.at[direction, hop - 1, p],
            device_id={"row": (ahead, behind)[direction]},
            device_id_type=MESH,
        )

    def across(key, p, source):
        part = gathered.at[source, pl.ds(p * z.piece, z.piece)]
        return pltpu.make_async_remote_copy(
            src_ref=part,
            dst_ref=part,
            send_sem=sib_send.at[key, p],
            recv_sem=sib_recv.at[key, p],
            device_id={"row": sibling},
            device_id_type=MESH,
        )

    def to_owner(k):
        return pltpu.make_async_remote_copy(
            src_ref=packed.at[lax.rem(me + k, z.n)],
            dst_ref=left.at[me],
            send_sem=left_send.at[k],
            recv_sem=left_recv.at[k],
            device_id={"row": lax.rem(me + k, z.n)},
            device_id_type=MESH,
        )

    started = []

    def start(copy):
        copy.start()
        started.append(copy)

    def travels(direction, hop, wave):
        return hop < z.hops or (hop == z.hops and wave == direction)

    def send_own(wave):
        for direction in range(2):
            if travels(direction, 1, wave):
                start(ring(direction, 1, wave, me))
        start(across(0, wave, me))

    def pass_on(wave, hop):
        arrived = []
        for direction in range(2):
            if not travels(direction, hop, wave):
                continue
            source = device_at(place + (hop if direction else z.chips - hop))
            ring(direction, hop, wave, source).wait_recv()
            if travels(direction, hop + 1, wave):
                start(ring(direction, hop + 1, wave, source))
            key = hop if direction == 0 or hop == z.hops else z.hops + hop
            arrived.append(across(key, wave, source))
        for copy in arrived:
            start(copy)

    def wait_across(wave):
        for key in range(z.chips):
            step = key if key <= z.hops else z.hops - key
            source = device_at(place - step + z.chips) + 1 - 2 * core
            across(key, wave, source).wait_recv()

    for load in loads:
        load.wait()
    w1t = jnp.concatenate([w1[...]] * z.pack, axis=0)
    b1_wide = jnp.concatenate([b1[...]] * z.pack, axis=1)
    eye = lax.broadcasted_iota(jnp.int32, (z.width, z.width), 0) == lax.broadcasted_iota(
        jnp.int32, (z.width, z.width), 1
    )
    b2_tall = jnp.sum(jnp.where(eye, b2[...], 0.0), axis=1, keepdims=True)
    params = (w1t, b1_wide, w2[...], b2_tall, scale[...], shift[...])
    rows = z.piece
    for wave in range(z.waves):
        x_loads[wave].wait()
        project(z, wave, x, params, wide, tall)
        part = wide[pl.ds(wave * rows * ROWS16, rows * ROWS16), :]
        gathered[me, pl.ds(wave * rows, rows)] = part.reshape(rows, ROWS16, LANES).astype(jnp.bfloat16)
        if wave == 0:
            pl.semaphore_wait(barrier, z.n - 1)
        send_own(wave)
    pass_on(0, 1)
    pack_left(z, tall, flat, packed)
    pass_on(1, 1)
    for k in range(1, z.n):
        start(to_owner(k))
    left[me] = packed[me]
    turn_weights(z, w, wide_w, wt)
    for hop in range(2, z.hops):
        for wave in range(z.waves):
            pass_on(wave, hop)
    for k in range(1, z.n):
        pltpu.make_async_remote_copy(
            src_ref=packed.at[me],
            dst_ref=left.at[lax.rem(me - k + z.n, z.n)],
            send_sem=left_send.at[k],
            recv_sem=left_recv.at[k],
            device_id={"row": lax.rem(me + k, z.n)},
            device_id_type=MESH,
        ).wait_recv()
    spread_left(z, left, a)
    pass_on(0, z.hops)
    pass_on(1, z.hops)

    for wave in range(z.waves):
        wait_across(wave)
        for at in range(z.per_wave):
            c = wave * z.per_wave + at
            for u in range(2):
                outer_part(z, c, u, a, gathered, held)
            for u in range(2):
                map_part(z, c, u, inverse, wt, bias, held, out_ref)
    for copy in started:
        copy.wait_send()


def solution(mesh):
    n = mesh.shape["row"]
    vmem = pl.BlockSpec(memory_space=pltpu.VMEM)

    def local(x, scale, shift, w1, b1, w2, b2, w, bias):
        z = Sizes(n, x.shape[0], x.shape[1], w1.shape[1], w.shape[1])
        inverse = 1.0 / (n * x.shape[0])
        pieces = z.waves
        operands = (
            x, scale.reshape(1, -1), shift.reshape(1, -1), w1.T, b1.reshape(1, -1),
            w2.T, b2.reshape(1, -1), w, bias.reshape(1, -1),
        )
        dma = pltpu.SemaphoreType.DMA
        room = 24 if z.n <= 16 else 48
        bf16, f32 = jnp.bfloat16, jnp.float32
        return pl.pallas_call(
            functools.partial(kernel, z, inverse),
            out_shape=jax.ShapeDtypeStruct((z.own, z.res, z.cz), bf16),
            in_specs=[pl.BlockSpec(memory_space=pltpu.HBM)] * 9,
            out_specs=vmem,
            scratch_shapes=[pltpu.VMEM(o.shape, o.dtype) for o in operands]
            + [
                pltpu.VMEM((z.tiles * ROWS16, LANES), f32),
                pltpu.VMEM((z.seqs * z.res, LANES), f32),
                pltpu.VMEM((n * z.q * ROWS16, LANES), f32),
                pltpu.VMEM((n, z.q, ROWS16, LANES), bf16),
                pltpu.VMEM((n, z.q, ROWS16, LANES), bf16),
                pltpu.VMEM((n, z.tiles, ROWS16, LANES), bf16),
                pltpu.VMEM(w.shape, f32),
                pltpu.VMEM((z.cz, w.shape[0]), bf16),
                pltpu.VMEM((z.parts * z.own * z.width, z.k), bf16),
                pltpu.VMEM((z.own // 2, z.width * z.width, 2 * LANES), bf16),
                dma((9 + z.waves,)),
                dma((2, z.hops, pieces)),
                dma((2, z.hops, pieces)),
                dma((z.chips, pieces)),
                dma((z.chips, pieces)),
                dma((n,)),
                dma((n,)),
            ],
            compiler_params=pltpu.CompilerParams(
                vmem_limit_bytes=room * 2**20, collective_id=0, has_side_effects=True
            ),
        )(*operands)

    in_specs = (P(("groups", "row"), None, None), P(), P(), P(), P(), P(), P(), P(), P())
    return jax.shard_map(
        local,
        mesh=mesh,
        in_specs=in_specs,
        out_specs=P(("groups", "row"), None, None),
        check_vma=False,
    )
```
